512 devices in a mesh: ep: 64 (over y, z_lo, core), dp: 8 (over z_hi, x).
Axes of the slice: x: 4, y: 4, z: 16 (z_hi: 2, z_lo: 8; z = z_hi * 8 + z_lo), core: 2. Of those that a mesh axis runs over, the one named last changes fastest.
Arguments:
- hidden: bfloat16 [2, 16384, 2048], P(None, ('ep', 'dp')), may hold values from -6 to 6
- norm_gain: bfloat16 [2048], replicated, may hold values from 0.5 to 1.5
- gate_weights: float32 [2, 16384, 8], P(None, ('ep', 'dp')), may hold values from 0.05 to 1
- routes: int32 [2, 16384, 8], P(None, ('ep', 'dp')), may hold values from 0 to 63, as said below
- replica_pick: int32 [2, 16384, 8], P(None, ('ep', 'dp')), may hold values from 0 to 4095
- trainer_experts: int32 [64], replicated, may hold values from 0 to 63, each once
- hot_experts: int32 [3], replicated, may hold values from 0 to 63, as said below
- replica_hot: int32 [64], replicated, may hold values from 0 to 2, as said below
- w_gate: bfloat16 [64, 2048, 384], P('ep', 'dp'), may hold values from -0.125 to 0.125
- w_up: bfloat16 [64, 2048, 384], P('ep', 'dp'), may hold values from -0.125 to 0.125
- w_down: bfloat16 [64, 384, 2048], P('ep', None, 'dp'), may hold values from -0.3125 to 0.3125
- queries: bfloat16 [2, 16384, 4096], P(None, ('ep', 'dp')), may hold values from -6 to 6
- key_cache: bfloat16 [16384, 32, 512], P(('ep', 'dp')), may hold values from -6 to 6
- value_cache: bfloat16 [16384, 32, 512], P(('ep', 'dp')), may hold values from -6 to 6
- new_keys: bfloat16 [2, 16384, 512], P(None, ('ep', 'dp')), may hold values from -6 to 6
- new_values: bfloat16 [2, 16384, 512], P(None, ('ep', 'dp')), may hold values from -6 to 6
- cache_lengths: int32 [16384], P(('ep', 'dp')), may hold values from 2 to 32, as said below
Outputs:
- mixed: bfloat16 [2, 16384, 2048], P(None, ('ep', 'dp'))
- context: bfloat16 [2, 16384, 4096], P(None, ('ep', 'dp'))
The draws below stay inside these ranges and needn't reach their ends.
Inputs may be any that keep to these rules, and one draw needn't show every extreme that they name: Trainer index p holds expert trainer_experts[p]; each expert once. `hot_experts`: 3 different experts, among them expert 0 and expert 64 - 1. `replica_hot`: every entry of hot_experts is named by some index. `cache_lengths`: the 32 sequences of each device include one with 32 live entries. `routes`: each row names 8 different experts; every expert is named by some row.
All inputs are finite; a program needn't handle non-finite values.
Results may differ from the reference program's by a relative error of at most 0.001.
The reference program's roundings to bfloat16 on the way count: a program that leaves them out, or rounds other values in their place, can miss the bound.
Values may be sent and summed in bfloat16 or wider, within the bound.
A program may use at most 64 MiB of HBM per device.

```python
import math
import jax
import jax.numpy as jnp
from jax import lax

D = 2048
FF = 384
HEADS = 32
KV_HEADS = 4
HEAD = 128
TOP = 8
CAP = 3
SLOTS = 2
HOT = 3
STEPS = 2
TOK_DEV = 32
CACHE = 32
EXPERTS = 64
TOKENS = 16384
N_EP = 64


def hot_choice(key):
    picked = jax.random.permutation(jax.random.fold_in(key, 3), EXPERTS)[:HOT].astype(jnp.int32)
    largest = jnp.max(picked)
    picked = jnp.where(picked == largest, EXPERTS - 1, picked)
    smallest = jnp.min(picked)
    picked = jnp.where(picked == smallest, 0, picked)
    return picked.astype(jnp.int32)


def draw_hot_experts(key, part):
    return hot_choice(key)


def draw_routes(key, part):
    hot_ids = hot_choice(key)
    expert_ids = jnp.arange(EXPERTS, dtype=jnp.int32)
    hot_mask = jnp.sum((expert_ids[:, None] == hot_ids[None, :]).astype(jnp.int32), axis=1)
    base_scores = jax.random.randint(jax.random.fold_in(key, 21), (STEPS, TOKENS, EXPERTS), 0, 65536)
    lucky = (jax.random.randint(jax.random.fold_in(key, 22), (STEPS, TOKENS, EXPERTS), 0, 10) < 9).astype(jnp.int32)
    scores = (base_scores + hot_mask[None, None, :] * lucky * 65536) * EXPERTS + expert_ids[None, None, :]
    return jax.lax.top_k(scores.astype(jnp.int32), TOP)[1].astype(jnp.int32)


def draw_replica_hot(key, part):
    base_key = jax.random.fold_in(key, 4)
    keys_four = jax.random.split(base_key, 4)
    factor_one = jax.random.randint(keys_four[0], (EXPERTS,), 0, HOT)
    factor_two = jax.random.randint(keys_four[1], (EXPERTS,), 0, HOT)
    skewed = factor_one * factor_two // HOT
    position = jnp.arange(EXPERTS)
    skewed = jnp.where(position < HOT, position, skewed)
    relabel = jax.random.permutation(keys_four[2], HOT)
    labelled = relabel[skewed]
    return labelled[jax.random.permutation(keys_four[3], EXPERTS)].astype(jnp.int32)


def draw_cache_lengths(key, part):
    lengths = jax.random.randint(jax.random.fold_in(key, 5), (TOKENS,), 2, CACHE + 1)
    block_pick = jax.random.randint(jax.random.fold_in(key, 6), (TOKENS // TOK_DEV,), 0, TOK_DEV)
    longest = jnp.repeat(block_pick, TOK_DEV) == jnp.arange(TOKENS) % TOK_DEV
    return jnp.where(longest, CACHE, lengths).astype(jnp.int32)


def draw_key_cache(key, part):
    noise = jnp.clip(jax.random.normal(jax.random.fold_in(key, 11), (TOKENS, CACHE, KV_HEADS * HEAD), jnp.float32), -6.0, 6.0)
    return noise.astype(jnp.bfloat16)


def draw_queries(key, part):
    noise = jnp.clip(jax.random.normal(jax.random.fold_in(key, 13), (STEPS, TOKENS, HEADS * HEAD), jnp.float32), -6.0, 6.0)
    return noise.astype(jnp.bfloat16)


def set_ends(drawn, rng, low, high):
    place = [jax.random.randint(jax.random.fold_in(rng, axis), (), 0, length) for axis, length in enumerate(drawn.shape)]
    widest = drawn.shape.index(max(drawn.shape))
    beside = place[:widest] + [(place[widest] + 1) % drawn.shape[widest]] + place[widest + 1:]
    return drawn.at[tuple(place)].set(low).at[tuple(beside)].set(high)


def shard_levels(own_key, shape, cuts, low, top_value):
    def one(dim, blocks):
        heights = jax.random.uniform(jax.random.fold_in(jax.random.fold_in(own_key, 6), dim), (blocks,), jnp.float32, low / len(cuts), top_value / len(cuts))
        return jnp.repeat(jnp.exp(heights), shape[dim] // blocks).reshape((-1,) + (1,) * (len(shape) - dim - 1))

    gain = one(*cuts[0])
    for cut in cuts[1:]:
        gain = gain * one(*cut)
    return gain


def scatter_about(rng, extent, scale, reach, cuts=(), kind=jnp.bfloat16):
    drawn = scale * jax.random.normal(rng, extent, jnp.float32)
    if cuts:
        drawn = drawn * shard_levels(rng, extent, cuts, -0.22, 0.18)
    return jnp.clip(drawn, -reach, reach).astype(kind)


def setup_inputs(seed: int = 0) -> dict:
    seeds = jax.random.split(jax.random.key(seed), 18)
    return {
        "hidden": scatter_about(seeds[0], (STEPS, TOKENS, D), 1.0, 6.0, ((1, 512),)),
        "norm_gain": jnp.clip(1.0 + 0.1 * jax.random.normal(seeds[1], (D,), jnp.float32), 0.5, 1.5).astype(jnp.bfloat16),
        "gate_weights": jnp.clip(jnp.exp(math.log(1.0) - 2.9957323 * jax.random.uniform(seeds[2], (STEPS, TOKENS, TOP), jnp.float32) ** shard_levels(seeds[2], (STEPS, TOKENS, TOP), ((1, 512),), -0.2, 0.2)), 0.05, 1.0),
        "routes": draw_routes(jax.random.fold_in(seeds[17], 71), 0),
        "replica_pick": set_ends(jax.random.randint(seeds[4], (STEPS, TOKENS, TOP), 0, 64 * EXPERTS), jax.random.fold_in(seeds[4], 1), 0, (64 * EXPERTS) - 1).astype(jnp.int32),
        "trainer_experts": jax.random.permutation(seeds[5], EXPERTS).astype(jnp.int32),
        "hot_experts": draw_hot_experts(jax.random.fold_in(seeds[17], 71), 0),
        "replica_hot": draw_replica_hot(jax.random.fold_in(seeds[17], 71), 0),
        "w_gate": scatter_about(seeds[8], (EXPERTS, D, FF), D ** -0.5, 0.125, ((0, 64), (1, 8))),
        "w_up": scatter_about(seeds[9], (EXPERTS, D, FF), D ** -0.5, 0.125, ((0, 64), (1, 8))),
        "w_down": scatter_about(seeds[10], (EXPERTS, FF, D), FF ** -0.5, 0.3125, ((0, 64), (2, 8))),
        "queries": draw_queries(jax.random.fold_in(seeds[17], 71), 0),
        "key_cache": draw_key_cache(jax.random.fold_in(seeds[17], 71), 0),
        "value_cache": scatter_about(seeds[13], (TOKENS, CACHE, KV_HEADS * HEAD), 1.0, 6.0, ((0, 512),)),
        "new_keys": scatter_about(seeds[14], (STEPS, TOKENS, KV_HEADS * HEAD), 1.0, 6.0, ((1, 512),)),
        "new_values": scatter_about(seeds[15], (STEPS, TOKENS, KV_HEADS * HEAD), 1.0, 6.0, ((1, 512),)),
        "cache_lengths": draw_cache_lengths(jax.random.fold_in(seeds[17], 71), 0),
    }


norm_epsilon = 1e-06

def scaled_norm(hidden_rows, norm_gain):
    values = hidden_rows.astype(jnp.float32)
    mean_square = lax.optimization_barrier(jnp.mean(values * values, axis=-1, keepdims=True))
    return (values * lax.rsqrt(mean_square + norm_epsilon) * norm_gain.astype(jnp.float32)).astype(jnp.bfloat16)

def attend_block(inputs, step_index):
    query_rows, cached_keys, cached_values, fresh_keys, fresh_values, lengths = inputs
    rows_here = query_rows.shape[0]
    grouped = query_rows.astype(jnp.float32).reshape(rows_here, KV_HEADS, HEADS // KV_HEADS, HEAD)
    keys_cached = cached_keys.astype(jnp.float32).reshape(rows_here, CACHE, KV_HEADS, HEAD)
    values_cached = cached_values.astype(jnp.float32).reshape(rows_here, CACHE, KV_HEADS, HEAD)
    keys_fresh = fresh_keys.astype(jnp.float32).reshape(rows_here, STEPS, KV_HEADS, HEAD)
    values_fresh = fresh_values.astype(jnp.float32).reshape(rows_here, STEPS, KV_HEADS, HEAD)
    score_scale = 1.0 / math.sqrt(HEAD)
    cache_scores = jnp.einsum('rkgh,rckh->rkgc', grouped, keys_cached) * score_scale
    fresh_scores = jnp.einsum('rkgh,rskh->rkgs', grouped, keys_fresh) * score_scale
    cache_mask = (jnp.arange(CACHE, dtype=jnp.int32)[None, :] < lengths[:, None])[:, None, None, :]
    fresh_mask = (jnp.arange(STEPS, dtype=jnp.int32) <= step_index)[None, None, None, :]
    row_max = jnp.maximum(lax.optimization_barrier(jnp.max(jnp.where(cache_mask, cache_scores, -1e+30), axis=-1)), lax.optimization_barrier(jnp.max(jnp.where(fresh_mask, fresh_scores, -1e+30), axis=-1)))
    cache_exp = jnp.where(cache_mask, jnp.exp(cache_scores - row_max[..., None]), 0.0)
    fresh_exp = jnp.where(fresh_mask, jnp.exp(fresh_scores - row_max[..., None]), 0.0)
    row_total = lax.optimization_barrier(jnp.sum(cache_exp, axis=-1)) + lax.optimization_barrier(jnp.sum(fresh_exp, axis=-1))
    cache_probs = (cache_exp / row_total[..., None]).astype(jnp.bfloat16).astype(jnp.float32)
    fresh_probs = (fresh_exp / row_total[..., None]).astype(jnp.bfloat16).astype(jnp.float32)
    summed = jnp.einsum('rkgc,rckh->rkgh', cache_probs, values_cached) + jnp.einsum('rkgs,rskh->rkgh', fresh_probs, values_fresh)
    return summed.astype(jnp.bfloat16).reshape(rows_here, HEADS * HEAD)

def reference(hidden, norm_gain, gate_weights, routes, replica_pick, trainer_experts, hot_experts, replica_hot, w_gate, w_up, w_down, queries, key_cache, value_cache, new_keys, new_values, cache_lengths):
    device_ids = jnp.arange(N_EP, dtype=jnp.int32)
    expert_ids = jnp.arange(EXPERTS, dtype=jnp.int32)
    home_device = lax.optimization_barrier(jnp.sum(jnp.where(trainer_experts[None, :] == expert_ids[:, None], device_ids[None, :], 0), axis=1)).astype(jnp.int32)
    hosted = hot_experts[replica_hot]
    is_replica = (hosted[None, :] == expert_ids[:, None]).astype(jnp.int32)
    replica_order = (jnp.cumsum(is_replica, axis=1) * is_replica).astype(jnp.int32)
    copies = (1 + lax.optimization_barrier(jnp.sum(is_replica, axis=1))).astype(jnp.int32)
    slot_count = N_EP * SLOTS
    buffer_rows = slot_count * CAP
    blocks = TOKENS // TOK_DEV
    entries = TOK_DEV * TOP
    block_ids = jnp.broadcast_to(jnp.arange(blocks, dtype=jnp.int32)[:, None], (blocks, entries))
    token_of_entry = block_ids * TOK_DEV + jnp.arange(entries, dtype=jnp.int32)[None, :] // TOP
    mixed_steps = []
    context_steps = []
    for step_index in range(STEPS):
        normed = scaled_norm(hidden[step_index], norm_gain)
        weights_top = gate_weights[step_index]
        gates = (weights_top / lax.optimization_barrier(jnp.sum(weights_top, axis=-1, keepdims=True))).astype(jnp.bfloat16)
        chosen = routes[step_index].reshape(blocks, entries)
        replica_picks = replica_pick[step_index].reshape(blocks, entries)
        replica_index = (replica_picks % copies[chosen]).astype(jnp.int32)
        matches = replica_order[chosen] == replica_index[..., None]
        replica_device = lax.optimization_barrier(jnp.sum(jnp.where(matches, device_ids, 0), axis=-1)).astype(jnp.int32)
        target = jnp.where(replica_index == 0, home_device[chosen], replica_device)
        slot_index = (target * SLOTS + (replica_index > 0).astype(jnp.int32)).astype(jnp.int32)
        onehot = (slot_index[..., None] == jnp.arange(slot_count, dtype=jnp.int32)).astype(jnp.int32)
        slot_rank = (lax.optimization_barrier(jnp.sum(jnp.cumsum(onehot, axis=1) * onehot, axis=-1)) - 1).astype(jnp.int32)
        is_kept = slot_rank < CAP
        row_index = jnp.where(is_kept, slot_index * CAP + slot_rank, buffer_rows).astype(jnp.int32)
        token_table = jnp.zeros((blocks, buffer_rows), jnp.int32).at[block_ids, row_index].set(token_of_entry, mode='drop')
        gate_table = jnp.zeros((blocks, buffer_rows), jnp.float32).at[block_ids, row_index].set(gates.reshape(blocks, entries).astype(jnp.float32), mode='drop')
        token_table = token_table.reshape(blocks, slot_count, CAP).transpose(1, 0, 2).reshape(slot_count, blocks * CAP)
        gate_table = gate_table.reshape(blocks, slot_count, CAP).transpose(1, 0, 2).reshape(slot_count, blocks * CAP)

        def slot_body(summed, inputs):
            slot_tokens, slot_gates, slot_number = inputs
            owner_device = slot_number // SLOTS
            expert = jnp.where(slot_number % SLOTS == 0, trainer_experts[owner_device], hosted[owner_device])
            source = home_device[expert]
            rows_in = normed[slot_tokens]
            gate_part = jnp.dot(rows_in, w_gate[source], preferred_element_type=jnp.float32)
            up_part = jnp.dot(rows_in, w_up[source], preferred_element_type=jnp.float32)
            hidden_units = (jax.nn.silu(gate_part) * up_part).astype(jnp.bfloat16)
            result = jnp.dot(hidden_units, w_down[source], preferred_element_type=jnp.float32).astype(jnp.bfloat16)
            summed = summed.at[slot_tokens].add(slot_gates[:, None] * result.astype(jnp.float32))
            return (summed, None)
        summed, _ = lax.scan(slot_body, jnp.zeros((TOKENS, D), jnp.float32), (token_table, gate_table, jnp.arange(slot_count, dtype=jnp.int32)))
        mixed_steps.append((hidden[step_index].astype(jnp.float32) + summed).astype(jnp.bfloat16))
        block_inputs = (queries[step_index].reshape(blocks, TOK_DEV, HEADS * HEAD), key_cache.reshape(blocks, TOK_DEV, CACHE, KV_HEADS * HEAD), value_cache.reshape(blocks, TOK_DEV, CACHE, KV_HEADS * HEAD), jnp.swapaxes(new_keys, 0, 1).reshape(blocks, TOK_DEV, STEPS, KV_HEADS * HEAD), jnp.swapaxes(new_values, 0, 1).reshape(blocks, TOK_DEV, STEPS, KV_HEADS * HEAD), cache_lengths.reshape(blocks, TOK_DEV))
        attended = lax.map(lambda inputs: attend_block(inputs, step_index), block_inputs)
        context_steps.append(attended.reshape(TOKENS, HEADS * HEAD))
    return (jnp.stack(mixed_steps), jnp.stack(context_steps))
```

```python
import math

import jax
import jax.numpy as jnp
from jax import lax
from jax.experimental import pallas as pl
from jax.experimental.pallas import tpu as pltpu
from jax.sharding import PartitionSpec as P

HEADS = 32
KV_HEADS = 4
HEAD = 128
TOP = 8
CAP = 3
EXPERTS = 64
FF = 384
WIDTH = 2048
ROWS = 64
SEQS = 32
CACHE = 32
FRESH = 16
GROUP = 16
PIECE = 256
GU = 16
CHUNKS = 24
LAG = 4
MESH = pl.DeviceIdType.MESH
BF16 = jnp.bfloat16
F32 = jnp.float32

norm_epsilon = 1e-06


def div(a, b):
    return lax.div(jnp.int32(a), jnp.int32(b))


def rem(a, b):
    return lax.rem(jnp.int32(a), jnp.int32(b))


def kernel(
    te_ref,
    len_ref,
    t_ref,
    hid_ref,
    wg_ref,
    wu_ref,
    wd_ref,
    q_ref,
    kc_ref,
    vc_ref,
    nk_ref,
    nv_ref,
    mixed_ref,
    ctx_ref,
    wgu,
    wdn,
    tok,
    inner,
    gv,
    pbuf,
    qbuf,
    rbuf,
    cr,
    s1,
    s2,
    xs_sem,
    xr_sem,
    ring_s,
    ring_r,
    ag_s,
    ag_r,
    c_s,
    c_r,
    s1_s,
    s1_r,
    s2_s,
    s2_r,
):
    ep = lax.axis_index("ep")
    dp = lax.axis_index("dp")
    y, zl, c = div(ep, 16), rem(div(ep, 2), 8), rem(ep, 2)
    zh, x = div(dp, 4), rem(dp, 4)
    z = zh * 8 + zl
    rho = rem(z + 16 - x, 4)
    back = rem(4 - rho, 4)

    def dev(px, py, pz, pc):
        return ((py * 8 + rem(pz, 8)) * 2 + pc, div(pz, 8) * 4 + px)

    up, down = dev(x, y, rem(z + 1, 16), c), dev(x, y, rem(z + 15, 16), c)
    twin = dev(x, y, z, 1 - c)
    xpeer = [None] + [dev(rem(x + d, 4), y, z, c) for d in (1, 2, 3)]
    ypeer = [None] + [dev(x, rem(y + d, 4), z, c) for d in (1, 2, 3)]

    barrier = pltpu.get_barrier_semaphore()
    for other in [up, down, twin] + xpeer[1:] + ypeer[1:]:
        pl.semaphore_signal(barrier, inc=1, device_id=other, device_id_type=MESH)
    pl.semaphore_wait(barrier, 9)

    def remote(src, dst, ssem, rsem, to):
        return pltpu.make_async_remote_copy(
            src_ref=src, dst_ref=dst, send_sem=ssem, recv_sem=rsem, device_id=to, device_id_type=MESH
        )

    def part_ref(q, part, xs):
        e, d = rem(q, 2), div(q, 2) * 4 + xs
        if part < 2:
            return wgu.at[e, pl.ds(pl.multiple_of(d * PIECE, PIECE), PIECE), pl.ds(part * FF, FF)]
        return wdn.at[e, d]

    def chunk_ref(q, j, is_down):
        e, half = rem(q, 2), div(q, 2)
        jj = j - GU if is_down else j
        i = div(jj, 2) if is_down else div(jj, 4)
        order = i + div(i, 2) * (5 - 2 * i)
        d = half * 4 + rem(x + order, 4)
        sub = rem(jj, 2)
        if is_down:
            return wdn.at[e, d, pl.ds(pl.multiple_of(sub * 192, 192), 192)]
        part = rem(div(jj, 2), 2)
        rows = pl.ds(pl.multiple_of(d * PIECE + sub * 128, 128), 128)
        return wgu.at[e, rows, pl.ds(pl.multiple_of(part * FF, FF), FF)]

    near_q = rem(div(z + 16 - rho - x, 4), 4)
    near_dq = rem(div(z + 16 + back - x, 4), 4)
    far_q = rem(div(z + 12 - rho - x, 4), 4)
    far_dq = rem(div(z + 20 + back - x, 4), 4)
    opp_q = rem(div(z + 8 - rho - x, 4), 4)
    source = rho == 0

    def ring_copy(q, j, is_down, flow):
        block = chunk_ref(q, j, is_down)
        return remote(block, block, ring_s.at[flow, j], ring_r.at[q, j], up if flow % 2 == 0 else down)

    def near(j, is_down):
        @pl.when(source & (rem(j, 2) == 0))
        def _():
            jj = j - GU if is_down else j
            i = div(jj, 2) if is_down else div(jj, 4)
            order = i + div(i, 2) * (5 - 2 * i)
            xs = rem(x + order, 4)
            if is_down:
                block = part_ref(near_q, 2, xs)
                remote(block, block, xs_sem.at[2], xr_sem.at[2, xs], up).wait_recv()
            else:
                part = rem(div(jj, 2), 2)
                for p in range(2):

                    @pl.when(part == p)
                    def _():
                        block = part_ref(near_q, p, xs)
                        remote(block, block, xs_sem.at[p], xr_sem.at[p, xs], up).wait_recv()

        goes_up, goes_down = ring_copy(near_q, j, is_down, 0), ring_copy(near_dq, j, is_down, 1)

        @pl.when(jnp.logical_not(source))
        def _():
            goes_up.wait_recv()

        goes_up.start()

        @pl.when(jnp.logical_not(source))
        def _():
            goes_down.wait_recv()

        goes_down.start()

    def far(j, is_down):
        goes_up, goes_down = ring_copy(far_q, j, is_down, 2), ring_copy(far_dq, j, is_down, 3)
        goes_up.wait_recv()

        @pl.when((rho < 3) | (rem(j, 2) == 0))
        def _():
            goes_up.start()

        goes_down.wait_recv()

        @pl.when((back < 3) | (rem(j, 2) == 1))
        def _():
            goes_down.start()

    def opposite(j, is_down):
        @pl.when(source)
        def _():
            ring_copy(opp_q, j, is_down, 0).wait_recv()

    def tick(t):
        for step, first in ((near, 0), (far, LAG), (opposite, 2 * LAG)):

            @pl.when((t >= first) & (t < first + GU))
            def _():
                step(t - first, False)

            @pl.when((t >= first + GU) & (t < first + CHUNKS))
            def _():
                step(t - first, True)

    tok[c, y, x] = t_ref[...]
    token_x = [remote(t_ref, tok.at[c, y, x], ag_s.at[d - 1], ag_r.at[3 - d], xpeer[d]) for d in (1, 2, 3)]
    token_y = [
        remote(tok.at[c, y], tok.at[c, y], ag_s.at[2 + d], ag_r.at[6 - d], ypeer[d]) for d in (1, 2, 3)
    ]
    token_c = [remote(tok.at[c, r], tok.at[c, r], ag_s.at[6 + r], ag_r.at[6 + r], twin) for r in range(4)]

    column = rem(zl, 4)
    my_q = zh * 2 + div(zl, 4)
    parts = (wg_ref.at[0], wu_ref.at[0], wd_ref.at[0])

    @pl.when(x == column)
    def _():
        for p in range(3):
            pltpu.make_async_copy(parts[p], part_ref(my_q, p, x), xr_sem.at[p, x]).start()

    goes_to = dev(column, y, z, c)

    def hand(p):
        return remote(parts[p], part_ref(my_q, p, x), xs_sem.at[p], xr_sem.at[p, x], goes_to)

    def hand_start(p):
        @pl.when(x != column)
        def _():
            hand(p).start()

    hand_start(0)
    hand_start(1)
    for copy in token_x:
        copy.start()
    hand_start(2)

    score_scale = 1.0 / math.sqrt(HEAD)
    column_ids = lax.broadcasted_iota(jnp.int32, (KV_HEADS * GROUP, CACHE + FRESH), 1)
    row_step = rem(div(lax.broadcasted_iota(jnp.int32, (KV_HEADS * GROUP, CACHE + FRESH), 0), 8), 2)
    fresh_seen = (column_ids >= CACHE) & (column_ids - CACHE <= row_step)

    def attend(b):
        scores, values = [], []
        for h in range(KV_HEADS):
            lanes = slice(h * HEAD, (h + 1) * HEAD)
            keys = jnp.concatenate([kc_ref[b, :, lanes], nk_ref[b, :, lanes]], axis=0)
            values.append(jnp.concatenate([vc_ref[b, :, lanes], nv_ref[b, :, lanes]], axis=0))
            scores.append(
                lax.dot_general(
                    q_ref[b, h], keys, (((1,), (1,)), ((), ())), preferred_element_type=F32
                )
            )
        live = (column_ids < jnp.minimum(len_ref[b], CACHE)) | fresh_seen
        score = jnp.where(live, jnp.concatenate(scores, axis=0) * score_scale, -1e30)
        top = jnp.max(score, axis=1, keepdims=True)
        weight = jnp.where(live, jnp.exp(score - top), 0.0)
        probs = (weight / jnp.sum(weight, axis=1, keepdims=True)).astype(BF16)
        for h in range(KV_HEADS):
            ctx_ref[b, h] = jnp.dot(
                probs[h * GROUP : (h + 1) * GROUP], values[h], preferred_element_type=F32
            ).astype(BF16)

    def attend_tick(t, carry):
        tick(t)
        attend(2 * t)
        attend(2 * t + 1)
        return carry

    lax.fori_loop(0, 3, attend_tick, 0)
    for d in (1, 2, 3):
        token_x[d - 1].wait_recv()
    for copy in token_y:
        copy.start()
    lax.fori_loop(3, 12, attend_tick, 0)
    for copy in token_y:
        copy.wait_recv()
    for copy in token_c:
        copy.start()
    lax.fori_loop(12, 16, attend_tick, 0)

    def only_tick(t, carry):
        tick(t)
        return carry

    lax.fori_loop(16, GU + 2 * LAG, only_tick, 0)
    for copy in token_c:
        copy.wait_recv()

    lane = lax.broadcasted_iota(jnp.int32, (256, 128), 1)

    def project(e, i):
        core, row = div(i, 4), rem(i, 4)
        rows = tok[core, row, :, :, pl.ds(0, WIDTH)].reshape(256, WIDTH)
        both = jnp.dot(rows, wgu[e], preferred_element_type=F32)
        gate, upper = both[:, :FF], both[:, FF:]
        inner[e, i] = (gate / (1.0 + jnp.exp(-gate)) * upper).astype(BF16)
        table = tok[core, row, :, :, pl.ds(WIDTH, 128)].reshape(256, 128).astype(F32)
        expert = te_ref[(y * 8 + x + 4 * e) * 2 + c]
        mine = jnp.sum(jnp.where(lane == expert, table, 0.0), axis=1, keepdims=True)
        gv[e, i] = jnp.broadcast_to(mine, (256, 128))

    def project_tick(n, carry):
        tick(GU + 2 * LAG + n)
        project(0, n)
        project(1, n)
        return carry

    lax.fori_loop(0, 8, project_tick, 0)

    def core_copy(n):
        return remote(pbuf.at[n % 2, 1 - c], cr.at[n], c_s.at[n], c_r.at[n], twin)

    def expand(n):
        if n >= 2:
            core_copy(n - 2).wait_send()

        def tile(core, i, carry):
            k = core * 4 + i
            total = None
            for e in range(2):
                out = jnp.dot(inner[e, k], wdn[e, n], preferred_element_type=F32)
                share = jnp.concatenate([gv[e, k], gv[e, k]], axis=1)
                part = share * out.astype(BF16).astype(F32)
                total = part if total is None else total + part
            pbuf[n % 2, core, i] = total.reshape(4, ROWS, PIECE)
            return carry

        lax.fori_loop(0, 4, lambda i, k: tile(1 - c, i, k), 0)
        core_copy(n).start()
        lax.fori_loop(0, 4, lambda i, k: tile(c, i, k), 0)

    def first_copies(n):
        out = []
        for d in (1, 2, 3):
            if n % 2 == 0:
                src, to = qbuf.at[n % 2, :, rem(x + d, 4)], xpeer[d]
            else:
                src, to = qbuf.at[n % 2, rem(y + d, 4)], ypeer[d]
            out.append(remote(src, s1.at[n, 3 - d], s1_s.at[n, d - 1], s1_r.at[n, 3 - d], to))
        return out

    def second_copies(n):
        out = []
        for d in (1, 2, 3):
            if n % 2 == 0:
                src, to = rbuf.at[n % 2, rem(y + d, 4)], ypeer[d]
            else:
                src, to = rbuf.at[n % 2, rem(x + d, 4)], xpeer[d]
            out.append(remote(src, s2.at[n, 3 - d], s2_s.at[n, d - 1], s2_r.at[n, 3 - d], to))
        return out

    def core_add(n):
        core_copy(n).wait_recv()
        if n >= 2:
            for copy in first_copies(n - 2):
                copy.wait_send()

        def add(i, carry):
            qbuf[n % 2, i] = pbuf[n % 2, c, i] + cr[n, i]
            return carry

        lax.fori_loop(0, 4, add, 0)
        for copy in first_copies(n):
            copy.start()

    def first_add(n):
        for copy in first_copies(n):
            copy.wait_recv()
        if n >= 2:
            for copy in second_copies(n - 2):
                copy.wait_send()

        def add(i, carry):
            own = qbuf[n % 2, i, x] if n % 2 == 0 else qbuf[n % 2, y, i]
            rbuf[n % 2, i] = own + s1[n, 0, i] + s1[n, 1, i] + s1[n, 2, i]
            return carry

        lax.fori_loop(0, 4, add, 0)
        for copy in second_copies(n):
            copy.start()

    def finish(n):
        for copy in second_copies(n):
            copy.wait_recv()
        own = rbuf[n % 2, y if n % 2 == 0 else x]
        total = own + s2[n, 0] + s2[n, 1] + s2[n, 2]
        lanes = slice(n * PIECE, (n + 1) * PIECE)
        mixed_ref[:, lanes] = (hid_ref[:, lanes].astype(F32) + total).astype(BF16)

    pieces = WIDTH // PIECE
    for n in range(pieces + 3):
        if n < pieces:
            expand(n)
        if 1 <= n < pieces + 1:
            core_add(n - 1)
        if 2 <= n < pieces + 2:
            first_add(n - 2)
        if n >= 3:
            finish(n - 3)

    for n in (pieces - 2, pieces - 1):
        core_copy(n).wait_send()
        for copy in first_copies(n) + second_copies(n):
            copy.wait_send()
    for copy in token_x + token_y + token_c:
        copy.wait_send()

    @pl.when(x != column)
    def _():
        for p in range(3):
            hand(p).wait_send()

    def drain(j, is_down):
        ring_copy(near_q, j, is_down, 0).wait_send()
        ring_copy(near_dq, j, is_down, 1).wait_send()

        @pl.when((rho < 3) | (rem(j, 2) == 0))
        def _():
            ring_copy(far_q, j, is_down, 2).wait_send()

        @pl.when((back < 3) | (rem(j, 2) == 1))
        def _():
            ring_copy(far_dq, j, is_down, 3).wait_send()

    def drain_gu(j, carry):
        drain(j, False)
        return carry

    def drain_down(j, carry):
        drain(j, True)
        return carry

    lax.fori_loop(0, GU, drain_gu, 0)
    lax.fori_loop(GU, CHUNKS, drain_down, 0)


def scaled_norm(hidden_rows, norm_gain):
    values = hidden_rows.astype(F32)
    mean_square = jnp.mean(values * values, axis=-1, keepdims=True)
    return (values * lax.rsqrt(mean_square + norm_epsilon) * norm_gain.astype(F32)).astype(BF16)


def gate_table(gate_weights, routes, replica_pick, hot_experts, replica_hot):
    steps, tokens, _ = routes.shape
    lanes = jnp.arange(128, dtype=jnp.int32)
    hot_ids = jnp.arange(hot_experts.shape[0], dtype=jnp.int32)
    counts = jnp.sum((replica_hot[:, None] == hot_ids[None, :]).astype(jnp.int32), axis=0)
    copies = 1 + jnp.sum(jnp.where(hot_experts[:, None] == lanes[None, :], counts[:, None], 0), axis=0)
    gates = (gate_weights / jnp.sum(gate_weights, axis=-1, keepdims=True)).astype(BF16).astype(F32)
    here = routes[..., None] == lanes
    named = jnp.any(here, axis=2)
    pick = jnp.sum(jnp.where(here, replica_pick[..., None], 0), axis=2)
    gate = jnp.sum(jnp.where(here, gates[..., None], 0.0), axis=2)
    slot = jnp.where(named, pick % copies, -1)
    order = jnp.arange(tokens, dtype=jnp.int32)
    before = (order[None, :] < order[:, None])[None, :, :, None]
    rank = jnp.sum((before & (slot[:, None, :, :] == slot[:, :, None, :])).astype(jnp.int32), axis=2)
    return jnp.where(named & (rank < CAP), gate, 0.0).astype(BF16)


def body(
    hidden,
    norm_gain,
    gate_weights,
    routes,
    replica_pick,
    trainer_experts,
    hot_experts,
    replica_hot,
    w_gate,
    w_up,
    w_down,
    queries,
    key_cache,
    value_cache,
    new_keys,
    new_values,
    cache_lengths,
):
    steps, tokens, width = hidden.shape
    table = gate_table(gate_weights, routes, replica_pick, hot_experts, replica_hot)
    rows = jnp.concatenate([scaled_norm(hidden, norm_gain), table], axis=-1).reshape(ROWS, width + 128)
    grouped = (
        queries.reshape(steps, tokens, KV_HEADS, HEADS // KV_HEADS, HEAD)
        .transpose(1, 2, 0, 3, 4)
        .reshape(tokens, KV_HEADS, GROUP, HEAD)
    )
    pad = ((0, 0), (0, FRESH - steps), (0, 0))
    fresh_keys = jnp.pad(new_keys.transpose(1, 0, 2), pad)
    fresh_values = jnp.pad(new_values.transpose(1, 0, 2), pad)
    vmem = pl.BlockSpec(memory_space=pltpu.VMEM)
    smem = pl.BlockSpec(memory_space=pltpu.SMEM)
    hbm = pl.BlockSpec(memory_space=pl.ANY)
    dma = pltpu.SemaphoreType.DMA
    mixed, context = pl.pallas_call(
        kernel,
        out_shape=(
            jax.ShapeDtypeStruct((ROWS, width), BF16),
            jax.ShapeDtypeStruct((tokens, KV_HEADS, GROUP, HEAD), BF16),
        ),
        in_specs=[smem, smem, vmem, vmem, hbm, hbm, hbm, vmem, vmem, vmem, vmem, vmem],
        out_specs=(vmem, vmem),
        scratch_shapes=[
            pltpu.VMEM((2, WIDTH, 2 * FF), BF16),
            pltpu.VMEM((2, WIDTH // PIECE, FF, PIECE), BF16),
            pltpu.VMEM((2, 4, 4, ROWS, WIDTH + 128), BF16),
            pltpu.VMEM((2, 8, 256, FF), BF16),
            pltpu.VMEM((2, 8, 256, 128), F32),
            pltpu.VMEM((2, 2, 4, 4, ROWS, PIECE), F32),
            pltpu.VMEM((2, 4, 4, ROWS, PIECE), F32),
            pltpu.VMEM((2, 4, ROWS, PIECE), F32),
            pltpu.VMEM((8, 4, 4, ROWS, PIECE), F32),
            pltpu.VMEM((8, 3, 4, ROWS, PIECE), F32),
            pltpu.VMEM((8, 3, ROWS, PIECE), F32),
            dma((3,)),
            dma((3, 4)),
            dma((4, CHUNKS)),
            dma((4, CHUNKS)),
            dma((10,)),
            dma((10,)),
            dma((8,)),
            dma((8,)),
            dma((8, 3)),
            dma((8, 3)),
            dma((8, 3)),
            dma((8, 3)),
        ],
        compiler_params=pltpu.CompilerParams(
            collective_id=0, has_side_effects=True, vmem_limit_bytes=62 * 1024 * 1024
        ),
        cost_estimate=pl.CostEstimate(flops=20_000_000_000, bytes_accessed=8_000_000, transcendentals=3_000_000),
    )(
        trainer_experts,
        cache_lengths,
        rows,
        hidden.reshape(ROWS, width),
        w_gate,
        w_up,
        w_down,
        grouped,
        key_cache,
        value_cache,
        fresh_keys,
        fresh_values,
    )
    context = (
        context.reshape(tokens, KV_HEADS, steps, HEADS // KV_HEADS, HEAD)
        .transpose(2, 0, 1, 3, 4)
        .reshape(steps, tokens, HEADS * HEAD)
    )
    return mixed.reshape(steps, tokens, width), context


def solution(mesh):
    return jax.shard_map(
        body,
        mesh=mesh,
        in_specs=(
            P(None, ("ep", "dp"), None),
            P(),
            P(None, ("ep", "dp"), None),
            P(None, ("ep", "dp"), None),
            P(None, ("ep", "dp"), None),
            P(),
            P(),
            P(),
            P("ep", "dp", None),
            P("ep", "dp", None),
            P("ep", None, "dp"),
            P(None, ("ep", "dp"), None),
            P(("ep", "dp"), None, None),
            P(("ep", "dp"), None, None),
            P(None, ("ep", "dp"), None),
            P(None, ("ep", "dp"), None),
            P(("ep", "dp")),
        ),
        out_specs=(P(None, ("ep", "dp"), None), P(None, ("ep", "dp"), None)),
        check_vma=False,
    )
```

```python
import math

import jax
import jax.numpy as jnp
from jax import lax
from jax.experimental import pallas as pl
from jax.experimental.pallas import tpu as pltpu
from jax.sharding import PartitionSpec as P

HEADS = 32
KV_HEADS = 4
HEAD = 128
TOP = 8
CAP = 3
EXPERTS = 64
FF = 384
WIDTH = 2048
ROWS = 64
SEQS = 32
CACHE = 32
FRESH = 16
GROUP = 16
PIECE = 256
GU = 32
CHUNKS = 48
HOP = 2
FULL = GU + 8 * HOP
SPLIT = 512
DOWN_ORDER = (0, 4, 1, 5, 2, 6, 3, 7)
MESH = pl.DeviceIdType.MESH
BF16 = jnp.bfloat16
F32 = jnp.float32

norm_epsilon = 1e-06


def div(a, b):
    return lax.div(jnp.int32(a), jnp.int32(b))


def rem(a, b):
    return lax.rem(jnp.int32(a), jnp.int32(b))


def kernel(
    te_ref,
    len_ref,
    t_ref,
    hid_ref,
    wg_ref,
    wu_ref,
    wd_ref,
    q_ref,
    kc_ref,
    vc_ref,
    nk_ref,
    nv_ref,
    mixed_ref,
    ctx_ref,
    wgu,
    wdn,
    tok,
    acc,
    inner,
    gv,
    pbuf,
    qbuf,
    rbuf,
    cr,
    s1,
    s2,
    xs_sem,
    xr_sem,
    ring_s,
    ring_r,
    ag_s,
    ag_r,
    c_s,
    c_r,
    s1_s,
    s1_r,
    s2_s,
    s2_r,
):
    ep = lax.axis_index("ep")
    dp = lax.axis_index("dp")
    y, zl, c = div(ep, 16), rem(div(ep, 2), 8), rem(ep, 2)
    zh, x = div(dp, 4), rem(dp, 4)
    z = zh * 8 + zl
    rho = rem(z + 16 - x, 4)
    back = rem(4 - rho, 4)

    def dev(px, py, pz, pc):
        return ((py * 8 + rem(pz, 8)) * 2 + pc, div(pz, 8) * 4 + px)

    up, down = dev(x, y, rem(z + 1, 16), c), dev(x, y, rem(z + 15, 16), c)
    twin = dev(x, y, z, 1 - c)
    xpeer = [None] + [dev(rem(x + d, 4), y, z, c) for d in (1, 2, 3)]
    ypeer = [None] + [dev(x, rem(y + d, 4), z, c) for d in (1, 2, 3)]

    barrier = pltpu.get_barrier_semaphore()
    for other in [up, down, twin] + xpeer[1:] + ypeer[1:]:
        pl.semaphore_signal(barrier, inc=1, device_id=other, device_id_type=MESH)
    pl.semaphore_wait(barrier, 9)

    def remote(src, dst, ssem, rsem, to):
        return pltpu.make_async_remote_copy(
            src_ref=src, dst_ref=dst, send_sem=ssem, recv_sem=rsem, device_id=to, device_id_type=MESH
        )

    def part_ref(q, part, xs):
        e, d = rem(q, 2), div(q, 2) * 4 + xs
        if part < 2:
            return wgu.at[e, pl.ds(pl.multiple_of(d * PIECE, PIECE), PIECE), pl.ds(part * FF, FF)]
        return wdn.at[e, d]

    def place(j, is_down):
        if is_down:
            return div(j - GU, 4), 2, rem(j, 4)
        i = div(j, 8)
        return rem(x + i + div(i, 2) * (5 - 2 * i), 4), rem(div(j, 4), 2), rem(j, 4)

    def chunk_ref(q, j, is_down):
        e, half = rem(q, 2), div(q, 2)
        xs, part, sub = place(j, is_down)
        d = half * 4 + xs
        if is_down:
            return wdn.at[e, d, pl.ds(pl.multiple_of(sub * 96, 96), 96)]
        rows = pl.ds(pl.multiple_of(d * PIECE + sub * 64, 64), 64)
        return wgu.at[e, rows, pl.ds(pl.multiple_of(part * FF, FF), FF)]

    near_q = rem(div(z + 16 - rho - x, 4), 4)
    near_dq = rem(div(z + 16 + back - x, 4), 4)
    far_q = rem(div(z + 12 - rho - x, 4), 4)
    far_dq = rem(div(z + 20 + back - x, 4), 4)
    opp_q = rem(div(z + 8 - rho - x, 4), 4)
    source = rho == 0

    def ring_copy(q, j, is_down, flow):
        block = chunk_ref(q, j, is_down)
        ssem = ring_s.at[flow, int(is_down)]
        return remote(block, block, ssem, ring_r.at[q, j], up if flow % 2 == 0 else down)

    def near_up(j, is_down):
        xs, part, sub = place(j, is_down)

        @pl.when(source & (sub == 0))
        def _():
            if is_down:
                block = part_ref(near_q, 2, xs)
                remote(block, block, xs_sem.at[2], xr_sem.at[2, xs], up).wait_recv()
            else:
                for p in range(2):

                    @pl.when(part == p)
                    def _():
                        block = part_ref(near_q, p, xs)
                        remote(block, block, xs_sem.at[p], xr_sem.at[p, xs], up).wait_recv()

        copy = ring_copy(near_q, j, is_down, 0)

        @pl.when(jnp.logical_not(source))
        def _():
            copy.wait_recv()

        copy.start()

    def near_down(j, is_down):
        copy = ring_copy(near_dq, j, is_down, 1)

        @pl.when(jnp.logical_not(source))
        def _():
            copy.wait_recv()

        copy.start()

    def far_up(j, is_down):
        copy = ring_copy(far_q, j, is_down, 2)
        copy.wait_recv()

        @pl.when((rho < 3) | (rem(j, 2) == 0))
        def _():
            copy.start()

    def far_down(j, is_down):
        copy = ring_copy(far_dq, j, is_down, 3)
        copy.wait_recv()

        @pl.when((back < 3) | (rem(j, 2) == 1))
        def _():
            copy.start()

    def opposite(j, is_down):
        @pl.when(source)
        def _():
            ring_copy(opp_q, j, is_down, 0).wait_recv()

    steps = (
        (near_up, rho * HOP),
        (near_down, back * HOP),
        (far_up, (rho + 4) * HOP),
        (far_down, (back + 4) * HOP),
        (opposite, 8 * HOP),
    )

    def tick(t):
        for step, first in steps:

            @pl.when((t >= first) & (t < first + GU))
            def _():
                step(t - first, False)

            @pl.when((t >= first + GU) & (t < first + CHUNKS))
            def _():
                step(t - first, True)

    tok[c, y, x] = t_ref[...]
    first, rest = pl.ds(0, SPLIT), pl.ds(SPLIT, WIDTH + 128 - SPLIT)
    token_1, token_2 = [], []
    for d in (1, 2, 3):
        token_1.append(
            remote(t_ref.at[:, rest], tok.at[c, y, x, :, rest], ag_s.at[d - 1], ag_r.at[3 - d], xpeer[d])
        )
        token_1.append(
            remote(t_ref.at[:, first], tok.at[c, y, x, :, first], ag_s.at[2 + d], ag_r.at[6 - d], ypeer[d])
        )
        block = tok.at[c, y, :, :, rest]
        token_2.append(remote(block, block, ag_s.at[5 + d], ag_r.at[9 - d], ypeer[d]))
        block = tok.at[c, :, x, :, first]
        token_2.append(remote(block, block, ag_s.at[8 + d], ag_r.at[12 - d], xpeer[d]))
    token_c = [remote(tok.at[c, r], tok.at[c, r], ag_s.at[12 + r], ag_r.at[12 + r], twin) for r in range(4)]

    column = rem(zl, 4)
    my_q = zh * 2 + div(zl, 4)
    parts = (wg_ref.at[0], wu_ref.at[0], wd_ref.at[0])

    @pl.when(x == column)
    def _():
        for p in range(3):
            pltpu.make_async_copy(parts[p], part_ref(my_q, p, x), xr_sem.at[p, x]).start()

    goes_to = dev(column, y, z, c)

    def hand(p):
        return remote(parts[p], part_ref(my_q, p, x), xs_sem.at[p], xr_sem.at[p, x], goes_to)

    def hand_start(p):
        @pl.when(x != column)
        def _():
            hand(p).start()

    hand_start(0)
    hand_start(1)
    for copy in token_1:
        copy.start()

    score_scale = 1.0 / math.sqrt(HEAD)
    column_ids = lax.broadcasted_iota(jnp.int32, (KV_HEADS * GROUP, CACHE + FRESH), 1)
    row_step = rem(div(lax.broadcasted_iota(jnp.int32, (KV_HEADS * GROUP, CACHE + FRESH), 0), 8), 2)
    fresh_seen = (column_ids >= CACHE) & (column_ids - CACHE <= row_step)

    def attend(b):
        scores, values = [], []
        for h in range(KV_HEADS):
            lanes = slice(h * HEAD, (h + 1) * HEAD)
            keys = jnp.concatenate([kc_ref[b, :, lanes], nk_ref[b, :, lanes]], axis=0)
            values.append(jnp.concatenate([vc_ref[b, :, lanes], nv_ref[b, :, lanes]], axis=0))
            scores.append(
                lax.dot_general(
                    q_ref[b, h], keys, (((1,), (1,)), ((), ())), preferred_element_type=F32
                )
            )
        live = (column_ids < jnp.minimum(len_ref[b], CACHE)) | fresh_seen
        score = jnp.where(live, jnp.concatenate(scores, axis=0) * score_scale, -1e30)
        top = jnp.max(score, axis=1, keepdims=True)
        weight = jnp.where(live, jnp.exp(score - top), 0.0)
        probs = (weight / jnp.sum(weight, axis=1, keepdims=True)).astype(BF16)
        for h in range(KV_HEADS):
            ctx_ref[b, h] = jnp.dot(
                probs[h * GROUP : (h + 1) * GROUP], values[h], preferred_element_type=F32
            ).astype(BF16)

    def attend_tick(t, carry):
        tick(t)
        attend(t)
        return carry

    lax.fori_loop(0, 5, attend_tick, 0)
    for copy in token_1:
        copy.wait_recv()
    for copy in token_2:
        copy.start()
    lax.fori_loop(5, 10, attend_tick, 0)
    hand_start(2)
    lax.fori_loop(10, 26, attend_tick, 0)
    for copy in token_2:
        copy.wait_recv()
    for copy in token_c:
        copy.start()
    lax.fori_loop(26, SEQS, attend_tick, 0)
    for copy in token_c:
        copy.wait_recv()

    lane = lax.broadcasted_iota(jnp.int32, (256, 128), 1)

    def product(e, i, quarters):
        core, row = div(i, 4), rem(i, 4)
        total = None
        for quarter in quarters:
            xs = rem(x + (0, 1, 3, 2)[quarter], 4)
            for half in range(2):
                here = pl.ds(pl.multiple_of((half * 4 + xs) * PIECE, PIECE), PIECE)
                rows = tok[core, row, :, :, here].reshape(256, PIECE)
                part = jnp.dot(rows, wgu[e, here, :], preferred_element_type=F32)
                total = part if total is None else total + part
        return total

    def finish_inner(e, i, quarters):
        both = acc[e, i] + product(e, i, quarters)
        gate, upper = both[:, :FF], both[:, FF:]
        inner[e, i] = (gate / (1.0 + jnp.exp(-gate)) * upper).astype(BF16)

    def share(e, i):
        core, row = div(i, 4), rem(i, 4)
        table = tok[core, row, :, :, pl.ds(WIDTH, 128)].reshape(256, 128).astype(F32)
        expert = te_ref[(y * 8 + x + 4 * e) * 2 + c]
        mine = jnp.sum(jnp.where(lane == expert, table, 0.0), axis=1, keepdims=True)
        gv[e, i] = jnp.broadcast_to(mine, (256, 128))

    def first_half(n, carry):
        tick(SEQS + n)
        for e in range(2):
            share(e, n)
            acc[e, n] = product(e, n, (0, 1))
        return carry

    def third_quarter(n, carry):
        tick(SEQS + 8 + n)
        for e in range(2):
            acc[e, n] += product(e, n, (2,))
        return carry

    def last_quarter(n, carry):
        for e in range(2):
            finish_inner(e, n, (3,))
        tick(FULL + n)
        return carry

    lax.fori_loop(0, 8, first_half, 0)
    lax.fori_loop(0, 8, third_quarter, 0)
    lax.fori_loop(0, 8, last_quarter, 0)

    def core_copy(n):
        return remote(pbuf.at[n % 2, 1 - c], cr.at[n % 4], c_s.at[n], c_r.at[n], twin)

    def expand(n):
        if n >= 2:
            core_copy(n - 2).wait_send()

        def tile(core, i, carry):
            k = core * 4 + i
            total = None
            for e in range(2):
                out = jnp.dot(inner[e, k], wdn[e, DOWN_ORDER[n]], preferred_element_type=F32)
                weight = jnp.concatenate([gv[e, k], gv[e, k]], axis=1)
                part = weight * out.astype(BF16).astype(F32)
                total = part if total is None else total + part
            pbuf[n % 2, core, i] = total.reshape(4, ROWS, PIECE)
            return carry

        lax.fori_loop(0, 4, lambda i, k: tile(1 - c, i, k), 0)
        core_copy(n).start()
        if n < 4:
            tick(FULL + 8 + 2 * n)
        lax.fori_loop(0, 4, lambda i, k: tile(c, i, k), 0)
        if n < 4:
            tick(FULL + 9 + 2 * n)

    def first_copies(n):
        out = []
        for d in (1, 2, 3):
            for h in range(2):
                if h == 0:
                    src, to = qbuf.at[n % 2, h, :, rem(x + d, 4)], xpeer[d]
                else:
                    src, to = qbuf.at[n % 2, h, rem(y + d, 4)], ypeer[d]
                dst = s1.at[n % 4, h, 3 - d]
                out.append(remote(src, dst, s1_s.at[n, h, d - 1], s1_r.at[n, h, 3 - d], to))
        return out

    def second_copies(n):
        out = []
        for d in (1, 2, 3):
            for h in range(2):
                if h == 0:
                    src, to = rbuf.at[n % 2, h, rem(y + d, 4)], ypeer[d]
                else:
                    src, to = rbuf.at[n % 2, h, rem(x + d, 4)], xpeer[d]
                dst = s2.at[n % 4, h, 3 - d]
                out.append(remote(src, dst, s2_s.at[n, h, d - 1], s2_r.at[n, h, 3 - d], to))
        return out

    def core_add(n):
        core_copy(n).wait_recv()
        if n >= 2:
            for copy in first_copies(n - 2):
                copy.wait_send()

        def add(i, carry):
            for h in range(2):
                lanes = slice(h * 128, (h + 1) * 128)
                qbuf[n % 2, h, i] = pbuf[n % 2, c, i, :, :, lanes] + cr[n % 4, i, :, :, lanes]
            return carry

        lax.fori_loop(0, 4, add, 0)
        for copy in first_copies(n):
            copy.start()

    def first_add(n):
        for copy in first_copies(n):
            copy.wait_recv()
        if n >= 2:
            for copy in second_copies(n - 2):
                copy.wait_send()

        def add(i, carry):
            for h in range(2):
                own = qbuf[n % 2, h, i, x] if h == 0 else qbuf[n % 2, h, y, i]
                rbuf[n % 2, h, i] = own + s1[n % 4, h, 0, i] + s1[n % 4, h, 1, i] + s1[n % 4, h, 2, i]
            return carry

        lax.fori_loop(0, 4, add, 0)
        for copy in second_copies(n):
            copy.start()

    def finish(n):
        for copy in second_copies(n):
            copy.wait_recv()
        for h in range(2):
            own = rbuf[n % 2, h, y if h == 0 else x]
            total = own + s2[n % 4, h, 0] + s2[n % 4, h, 1] + s2[n % 4, h, 2]
            begin = DOWN_ORDER[n] * PIECE + h * 128
            lanes = slice(begin, begin + 128)
            mixed_ref[:, lanes] = (hid_ref[:, lanes].astype(F32) + total).astype(BF16)

    pieces = WIDTH // PIECE
    for n in range(pieces + 3):
        if n < pieces:
            expand(n)
        if 1 <= n < pieces + 1:
            core_add(n - 1)
        if 2 <= n < pieces + 2:
            first_add(n - 2)
        if n >= 3:
            finish(n - 3)

    for n in (pieces - 2, pieces - 1):
        core_copy(n).wait_send()
        for copy in first_copies(n) + second_copies(n):
            copy.wait_send()
    for copy in token_1 + token_2 + token_c:
        copy.wait_send()

    @pl.when(x != column)
    def _():
        for p in range(3):
            hand(p).wait_send()

    def drain(flow, is_down, halves):
        if is_down:
            block = wdn.at[0, pl.ds(0, 2 * halves)]
        else:
            block = wgu.at[0, pl.ds(0, 512 * halves)]
        remote(block, block, ring_s.at[flow, int(is_down)], ring_r.at[0, 0], up).wait_send()

    for is_down in (False, True):
        drain(0, is_down, 2)
        drain(1, is_down, 2)
        for flow, last in ((2, rho), (3, back)):

            @pl.when(last < 3)
            def _():
                drain(flow, is_down, 2)

            @pl.when(last == 3)
            def _():
                drain(flow, is_down, 1)


def scaled_norm(hidden_rows, norm_gain):
    values = hidden_rows.astype(F32)
    mean_square = jnp.mean(values * values, axis=-1, keepdims=True)
    return (values * lax.rsqrt(mean_square + norm_epsilon) * norm_gain.astype(F32)).astype(BF16)


def gate_table(gate_weights, routes, replica_pick, hot_experts, replica_hot):
    steps, tokens, _ = routes.shape
    lanes = jnp.arange(128, dtype=jnp.int32)
    hot_ids = jnp.arange(hot_experts.shape[0], dtype=jnp.int32)
    counts = jnp.sum((replica_hot[:, None] == hot_ids[None, :]).astype(jnp.int32), axis=0)
    copies = 1 + jnp.sum(jnp.where(hot_experts[:, None] == lanes[None, :], counts[:, None], 0), axis=0)
    gates = (gate_weights / jnp.sum(gate_weights, axis=-1, keepdims=True)).astype(BF16).astype(F32)
    here = routes[..., None] == lanes
    named = jnp.any(here, axis=2)
    pick = jnp.sum(jnp.where(here, replica_pick[..., None], 0), axis=2)
    gate = jnp.sum(jnp.where(here, gates[..., None], 0.0), axis=2)
    slot = jnp.where(named, pick % copies, -1)
    order = jnp.arange(tokens, dtype=jnp.int32)
    before = (order[None, :] < order[:, None])[None, :, :, None]
    rank = jnp.sum((before & (slot[:, None, :, :] == slot[:, :, None, :])).astype(jnp.int32), axis=2)
    return jnp.where(named & (rank < CAP), gate, 0.0).astype(BF16)


def body(
    hidden,
    norm_gain,
    gate_weights,
    routes,
    replica_pick,
    trainer_experts,
    hot_experts,
    replica_hot,
    w_gate,
    w_up,
    w_down,
    queries,
    key_cache,
    value_cache,
    new_keys,
    new_values,
    cache_lengths,
):
    steps, tokens, width = hidden.shape
    table = gate_table(gate_weights, routes, replica_pick, hot_experts, replica_hot)
    rows = jnp.concatenate([scaled_norm(hidden, norm_gain), table], axis=-1).reshape(ROWS, width + 128)
    grouped = (
        queries.reshape(steps, tokens, KV_HEADS, HEADS // KV_HEADS, HEAD)
        .transpose(1, 2, 0, 3, 4)
        .reshape(tokens, KV_HEADS, GROUP, HEAD)
    )
    pad = ((0, 0), (0, FRESH - steps), (0, 0))
    fresh_keys = jnp.pad(new_keys.transpose(1, 0, 2), pad)
    fresh_values = jnp.pad(new_values.transpose(1, 0, 2), pad)
    vmem = pl.BlockSpec(memory_space=pltpu.VMEM)
    smem = pl.BlockSpec(memory_space=pltpu.SMEM)
    hbm = pl.BlockSpec(memory_space=pl.ANY)
    dma = pltpu.SemaphoreType.DMA
    mixed, context = pl.pallas_call(
        kernel,
        out_shape=(
            jax.ShapeDtypeStruct((ROWS, width), BF16),
            jax.ShapeDtypeStruct((tokens, KV_HEADS, GROUP, HEAD), BF16),
        ),
        in_specs=[smem, smem, vmem, vmem, hbm, hbm, hbm, vmem, vmem, vmem, vmem, vmem],
        out_specs=(vmem, vmem),
        scratch_shapes=[
            pltpu.VMEM((2, WIDTH, 2 * FF), BF16),
            pltpu.VMEM((2, WIDTH // PIECE, FF, PIECE), BF16),
            pltpu.VMEM((2, 4, 4, ROWS, WIDTH + 128), BF16),
            pltpu.VMEM((2, 8, 256, 2 * FF), F32),
            pltpu.VMEM((2, 8, 256, FF), BF16),
            pltpu.VMEM((2, 8, 256, 128), F32),
            pltpu.VMEM((2, 2, 4, 4, ROWS, PIECE), F32),
            pltpu.VMEM((2, 2, 4, 4, ROWS, 128), F32),
            pltpu.VMEM((2, 2, 4, ROWS, 128), F32),
            pltpu.VMEM((4, 4, 4, ROWS, PIECE), F32),
            pltpu.VMEM((4, 2, 3, 4, ROWS, 128), F32),
            pltpu.VMEM((4, 2, 3, ROWS, 128), F32),
            dma((3,)),
            dma((3, 4)),
            dma((4, 2)),
            dma((4, CHUNKS)),
            dma((16,)),
            dma((16,)),
            dma((8,)),
            dma((8,)),
            dma((8, 2, 3)),
            dma((8, 2, 3)),
            dma((8, 2, 3)),
            dma((8, 2, 3)),
        ],
        compiler_params=pltpu.CompilerParams(
            collective_id=0, has_side_effects=True, vmem_limit_bytes=62 * 1024 * 1024
        ),
        cost_estimate=pl.CostEstimate(flops=20_000_000_000, bytes_accessed=8_000_000, transcendentals=3_000_000),
    )(
        trainer_experts,
        cache_lengths,
        rows,
        hidden.reshape(ROWS, width),
        w_gate,
        w_up,
        w_down,
        grouped,
        key_cache,
        value_cache,
        fresh_keys,
        fresh_values,
    )
    context = (
        context.reshape(tokens, KV_HEADS, steps, HEADS // KV_HEADS, HEAD)
        .transpose(2, 0, 1, 3, 4)
        .reshape(steps, tokens, HEADS * HEAD)
    )
    return mixed.reshape(steps, tokens, width), context


def solution(mesh):
    return jax.shard_map(
        body,
        mesh=mesh,
        in_specs=(
            P(None, ("ep", "dp"), None),
            P(),
            P(None, ("ep", "dp"), None),
            P(None, ("ep", "dp"), None),
            P(None, ("ep", "dp"), None),
            P(),
            P(),
            P(),
            P("ep", "dp", None),
            P("ep", "dp", None),
            P("ep", None, "dp"),
            P(None, ("ep", "dp"), None),
            P(("ep", "dp"), None, None),
            P(("ep", "dp"), None, None),
            P(None, ("ep", "dp"), None),
            P(None, ("ep", "dp"), None),
            P(("ep", "dp")),
        ),
        out_specs=(P(None, ("ep", "dp"), None), P(None, ("ep", "dp"), None)),
        check_vma=False,
    )
```

```python
import math

import jax
import jax.numpy as jnp
from jax import lax
from jax.experimental import pallas as pl
from jax.experimental.pallas import tpu as pltpu
from jax.sharding import PartitionSpec as P

HEADS = 32
KV_HEADS = 4
HEAD = 128
TOP = 8
CAP = 3
EXPERTS = 64
FF = 384
WIDTH = 2048
ROWS = 64
SEQS = 32
CACHE = 32
FRESH = 16
GROUP = 16
PIECE = 256
GU = 32
CHUNKS = 48
HOP = 2
FULL = GU + 8 * HOP
SPLIT = 512
DOWN_ORDER = (0, 4, 1, 5, 2, 6, 3, 7)
MESH = pl.DeviceIdType.MESH
BF16 = jnp.bfloat16
F32 = jnp.float32

norm_epsilon = 1e-06


def div(a, b):
    return lax.div(jnp.int32(a), jnp.int32(b))


def rem(a, b):
    return lax.rem(jnp.int32(a), jnp.int32(b))


def kernel(
    te_ref,
    len_ref,
    t_ref,
    hid_ref,
    wg_ref,
    wu_ref,
    wd_ref,
    q_ref,
    kc_ref,
    vc_ref,
    nk_ref,
    nv_ref,
    mixed_ref,
    ctx_ref,
    wgu,
    wdn,
    tok,
    acc,
    inner,
    gv,
    pbuf,
    qbuf,
    rbuf,
    cr,
    so,
    s1,
    s2,
    xs_sem,
    xr_sem,
    ring_s,
    ring_r,
    ag_s,
    ag_r,
    c_s,
    c_r,
    so_s,
    so_r,
    s1_s,
    s1_r,
    s2_s,
    s2_r,
):
    ep = lax.axis_index("ep")
    dp = lax.axis_index("dp")
    y, zl, c = div(ep, 16), rem(div(ep, 2), 8), rem(ep, 2)
    zh, x = div(dp, 4), rem(dp, 4)
    z = zh * 8 + zl
    rho = rem(z + 16 - x, 4)
    back = rem(4 - rho, 4)

    def dev(px, py, pz, pc):
        return ((py * 8 + rem(pz, 8)) * 2 + pc, div(pz, 8) * 4 + px)

    up, down = dev(x, y, rem(z + 1, 16), c), dev(x, y, rem(z + 15, 16), c)
    twin = dev(x, y, z, 1 - c)
    xpeer = [None] + [dev(rem(x + d, 4), y, z, c) for d in (1, 2, 3)]
    ypeer = [None] + [dev(x, rem(y + d, 4), z, c) for d in (1, 2, 3)]

    barrier = pltpu.get_barrier_semaphore()
    for other in [up, down, twin] + xpeer[1:] + ypeer[1:]:
        pl.semaphore_signal(barrier, inc=1, device_id=other, device_id_type=MESH)
    pl.semaphore_wait(barrier, 9)

    def remote(src, dst, ssem, rsem, to):
        return pltpu.make_async_remote_copy(
            src_ref=src, dst_ref=dst, send_sem=ssem, recv_sem=rsem, device_id=to, device_id_type=MESH
        )

    def part_ref(q, part, xs):
        e, d = rem(q, 2), div(q, 2) * 4 + xs
        if part < 2:
            return wgu.at[e, pl.ds(pl.multiple_of(d * PIECE, PIECE), PIECE), pl.ds(part * FF, FF)]
        return wdn.at[e, d]

    def place(j, is_down):
        if is_down:
            return div(j - GU, 4), 2, rem(j, 4)
        i = div(j, 8)
        return rem(x + i + div(i, 2) * (5 - 2 * i), 4), rem(div(j, 4), 2), rem(j, 4)

    def chunk_ref(q, j, is_down):
        e, half = rem(q, 2), div(q, 2)
        xs, part, sub = place(j, is_down)
        d = half * 4 + xs
        if is_down:
            return wdn.at[e, d, pl.ds(pl.multiple_of(sub * 96, 96), 96)]
        rows = pl.ds(pl.multiple_of(d * PIECE + sub * 64, 64), 64)
        return wgu.at[e, rows, pl.ds(pl.multiple_of(part * FF, FF), FF)]

    near_q = rem(div(z + 16 - rho - x, 4), 4)
    near_dq = rem(div(z + 16 + back - x, 4), 4)
    far_q = rem(div(z + 12 - rho - x, 4), 4)
    far_dq = rem(div(z + 20 + back - x, 4), 4)
    opp_q = rem(div(z + 8 - rho - x, 4), 4)
    source = rho == 0

    def ring_copy(q, j, is_down, flow):
        block = chunk_ref(q, j, is_down)
        ssem = ring_s.at[flow, int(is_down)]
        return remote(block, block, ssem, ring_r.at[q, j], up if flow % 2 == 0 else down)

    def near_up(j, is_down):
        xs, part, sub = place(j, is_down)

        @pl.when(source & (sub == 0))
        def _():
            if is_down:
                block = part_ref(near_q, 2, xs)
                remote(block, block, xs_sem.at[2], xr_sem.at[2, xs], up).wait_recv()
            else:
                for p in range(2):

                    @pl.when(part == p)
                    def _():
                        block = part_ref(near_q, p, xs)
                        remote(block, block, xs_sem.at[p], xr_sem.at[p, xs], up).wait_recv()

        copy = ring_copy(near_q, j, is_down, 0)

        @pl.when(jnp.logical_not(source))
        def _():
            copy.wait_recv()

        copy.start()

    def near_down(j, is_down):
        copy = ring_copy(near_dq, j, is_down, 1)

        @pl.when(jnp.logical_not(source))
        def _():
            copy.wait_recv()

        copy.start()

    def far_up(j, is_down):
        copy = ring_copy(far_q, j, is_down, 2)
        copy.wait_recv()

        @pl.when((rho < 3) | (rem(j, 2) == 0))
        def _():
            copy.start()

    def far_down(j, is_down):
        copy = ring_copy(far_dq, j, is_down, 3)
        copy.wait_recv()

        @pl.when((back < 3) | (rem(j, 2) == 1))
        def _():
            copy.start()

    def opposite(j, is_down):
        @pl.when(source)
        def _():
            ring_copy(opp_q, j, is_down, 0).wait_recv()

    steps = (
        (near_up, rho * HOP),
        (near_down, back * HOP),
        (far_up, (rho + 4) * HOP),
        (far_down, (back + 4) * HOP),
        (opposite, 8 * HOP),
    )

    def tick(t):
        for step, first in steps:

            @pl.when((t >= first) & (t < first + GU))
            def _():
                step(t - first, False)

            @pl.when((t >= first + GU) & (t < first + CHUNKS))
            def _():
                step(t - first, True)

    tok[c, y, x] = t_ref[...]
    first, rest = pl.ds(0, SPLIT), pl.ds(SPLIT, WIDTH + 128 - SPLIT)
    token_1, token_2 = [], []
    for d in (1, 2, 3):
        token_1.append(
            remote(t_ref.at[:, rest], tok.at[c, y, x, :, rest], ag_s.at[d - 1], ag_r.at[3 - d], xpeer[d])
        )
        token_1.append(
            remote(t_ref.at[:, first], tok.at[c, y, x, :, first], ag_s.at[2 + d], ag_r.at[6 - d], ypeer[d])
        )
        block = tok.at[c, y, :, :, rest]
        token_2.append(remote(block, block, ag_s.at[5 + d], ag_r.at[9 - d], ypeer[d]))
        block = tok.at[c, :, x, :, first]
        token_2.append(remote(block, block, ag_s.at[8 + d], ag_r.at[12 - d], xpeer[d]))
    token_c = [remote(tok.at[c, r], tok.at[c, r], ag_s.at[12 + r], ag_r.at[12 + r], twin) for r in range(4)]

    column = rem(zl, 4)
    my_q = zh * 2 + div(zl, 4)
    parts = (wg_ref.at[0], wu_ref.at[0], wd_ref.at[0])

    @pl.when(x == column)
    def _():
        for p in range(3):
            pltpu.make_async_copy(parts[p], part_ref(my_q, p, x), xr_sem.at[p, x]).start()

    goes_to = dev(column, y, z, c)

    def hand(p):
        return remote(parts[p], part_ref(my_q, p, x), xs_sem.at[p], xr_sem.at[p, x], goes_to)

    def hand_start(p):
        @pl.when(x != column)
        def _():
            hand(p).start()

    hand_start(0)
    hand_start(1)
    for copy in token_1:
        copy.start()

    score_scale = 1.0 / math.sqrt(HEAD)
    column_ids = lax.broadcasted_iota(jnp.int32, (KV_HEADS * GROUP, CACHE + FRESH), 1)
    row_step = rem(div(lax.broadcasted_iota(jnp.int32, (KV_HEADS * GROUP, CACHE + FRESH), 0), 8), 2)
    fresh_seen = (column_ids >= CACHE) & (column_ids - CACHE <= row_step)

    def attend(b):
        scores, values = [], []
        for h in range(KV_HEADS):
            lanes = slice(h * HEAD, (h + 1) * HEAD)
            keys = jnp.concatenate([kc_ref[b, :, lanes], nk_ref[b, :, lanes]], axis=0)
            values.append(jnp.concatenate([vc_ref[b, :, lanes], nv_ref[b, :, lanes]], axis=0))
            scores.append(
                lax.dot_general(
                    q_ref[b, h], keys, (((1,), (1,)), ((), ())), preferred_element_type=F32
                )
            )
        live = (column_ids < jnp.minimum(len_ref[b], CACHE)) | fresh_seen
        score = jnp.where(live, jnp.concatenate(scores, axis=0) * score_scale, -1e30)
        top = jnp.max(score, axis=1, keepdims=True)
        weight = jnp.where(live, jnp.exp(score - top), 0.0)
        probs = (weight / jnp.sum(weight, axis=1, keepdims=True)).astype(BF16)
        for h in range(KV_HEADS):
            ctx_ref[b, h] = jnp.dot(
                probs[h * GROUP : (h + 1) * GROUP], values[h], preferred_element_type=F32
            ).astype(BF16)

    def attend_tick(t, carry):
        tick(t)
        attend(t)
        return carry

    def only_tick(t, carry):
        tick(t)
        return carry

    lax.fori_loop(0, 14, attend_tick, 0)
    for copy in token_1:
        copy.wait_recv()
    for copy in token_2:
        copy.start()
    hand_start(2)
    lax.fori_loop(14, SEQS, attend_tick, 0)
    lax.fori_loop(SEQS, FULL - 12, only_tick, 0)
    for copy in token_2:
        copy.wait_recv()
    for copy in token_c:
        copy.start()
    lax.fori_loop(FULL - 12, FULL - 6, only_tick, 0)
    for copy in token_c:
        copy.wait_recv()

    lane = lax.broadcasted_iota(jnp.int32, (256, 128), 1)

    def product(e, i, quarters):
        core, row = div(i, 4), rem(i, 4)
        total = None
        for quarter in quarters:
            xs = rem(x + (0, 1, 3, 2)[quarter], 4)
            for half in range(2):
                here = pl.ds(pl.multiple_of((half * 4 + xs) * PIECE, PIECE), PIECE)
                rows = tok[core, row, :, :, here].reshape(256, PIECE)
                part = jnp.dot(rows, wgu[e, here, :], preferred_element_type=F32)
                total = part if total is None else total + part
        return total

    def finish_inner(e, i, quarters):
        both = acc[e, i] + product(e, i, quarters)
        gate, upper = both[:, :FF], both[:, FF:]
        inner[e, i] = (gate / (1.0 + jnp.exp(-gate)) * upper).astype(BF16)

    def share(e, i):
        core, row = div(i, 4), rem(i, 4)
        table = tok[core, row, :, :, pl.ds(WIDTH, 128)].reshape(256, 128).astype(F32)
        expert = te_ref[(y * 8 + x + 4 * e) * 2 + c]
        mine = jnp.sum(jnp.where(lane == expert, table, 0.0), axis=1, keepdims=True)
        gv[e, i] = jnp.broadcast_to(mine, (256, 128))

    def first_half(n, carry):
        tick(FULL - 6 + n)
        for i in range(2):
            for e in range(2):
                share(e, 2 * n + i)
                acc[e, 2 * n + i] = product(e, 2 * n + i, (0, 1))
        return carry

    def third_quarter(n, carry):
        tick(FULL - 2 + n)

        def rows(i, carry):
            for e in range(2):
                acc[e, i] += product(e, i, (2,))
            return carry

        lax.fori_loop(4 * n, 4 * n + 4, rows, 0)
        return carry

    def last_quarter(n, carry):
        for i in range(2):
            for e in range(2):
                finish_inner(e, 2 * n + i, (3,))
        tick(FULL + n)
        return carry

    lax.fori_loop(0, 4, first_half, 0)
    lax.fori_loop(0, 2, third_quarter, 0)
    lax.fori_loop(0, 4, last_quarter, 0)

    def core_copy(n):
        return remote(pbuf.at[n % 2, 1 - c], cr.at[n % 4], c_s.at[n], c_r.at[n], twin)

    def expand(n):
        if n >= 2:
            core_copy(n - 2).wait_send()

        def tile(core, i, carry):
            k = core * 4 + i
            total = None
            for e in range(2):
                out = jnp.dot(inner[e, k], wdn[e, DOWN_ORDER[n]], preferred_element_type=F32)
                weight = jnp.concatenate([gv[e, k], gv[e, k]], axis=1)
                part = weight * out.astype(BF16).astype(F32)
                total = part if total is None else total + part
            pbuf[n % 2, core, i] = total.reshape(4, ROWS, PIECE)
            return carry

        lax.fori_loop(0, 4, lambda i, k: tile(1 - c, i, k), 0)
        core_copy(n).start()
        if n < 6:
            tick(FULL + 4 + 2 * n)
        lax.fori_loop(0, 4, lambda i, k: tile(c, i, k), 0)
        if n < 6:
            tick(FULL + 5 + 2 * n)

    def block(n, h, k, rows):
        return qbuf.at[n % 3, h, rows, k] if h == 0 else qbuf.at[n % 3, h, k, rows]

    def along(h, d):
        return (rem(x + d, 4), xpeer[d]) if h == 0 else (rem(y + d, 4), ypeer[d])

    def opposite_copies(n):
        out = []
        for h in range(2):
            across, _ = along(h, 2)
            for side, d in ((0, 1), (1, 3)):
                src = block(n, h, across, pl.ds(2 * side, 2))
                dst = so.at[n % 4, h, side]
                out.append(remote(src, dst, so_s.at[n, h, side], so_r.at[n, h, side], along(h, d)[1]))
        return out

    def first_copies(n):
        out = []
        for h in range(2):
            for side, d in ((0, 1), (1, 3)):
                k, to = along(h, d)
                dst = s1.at[n % 4, h, side]
                out.append(
                    remote(block(n, h, k, pl.ds(0, 4)), dst, s1_s.at[n, h, side], s1_r.at[n, h, side], to)
                )
        return out

    def second_copies(n):
        out = []
        for d in (1, 2, 3):
            for h in range(2):
                if h == 0:
                    src, to = rbuf.at[n % 2, h, rem(y + d, 4)], ypeer[d]
                else:
                    src, to = rbuf.at[n % 2, h, rem(x + d, 4)], xpeer[d]
                dst = s2.at[n % 4, h, 3 - d]
                out.append(remote(src, dst, s2_s.at[n, h, d - 1], s2_r.at[n, h, 3 - d], to))
        return out

    def core_add(n):
        core_copy(n).wait_recv()
        if n >= 3:
            for copy in opposite_copies(n - 3) + first_copies(n - 3):
                copy.wait_send()

        def add(i, carry):
            for h in range(2):
                lanes = slice(h * 128, (h + 1) * 128)
                qbuf[n % 3, h, i] = pbuf[n % 2, c, i, :, :, lanes] + cr[n % 4, i, :, :, lanes]
            return carry

        lax.fori_loop(0, 4, add, 0)
        for copy in opposite_copies(n):
            copy.start()

    def opposite_add(n):
        for copy in opposite_copies(n):
            copy.wait_recv()
        for i in range(2):
            qbuf[n % 3, 0, i, rem(x + 1, 4)] += so[n % 4, 0, 0, i]
            qbuf[n % 3, 0, 2 + i, rem(x + 3, 4)] += so[n % 4, 0, 1, i]
            qbuf[n % 3, 1, rem(y + 1, 4), i] += so[n % 4, 1, 0, i]
            qbuf[n % 3, 1, rem(y + 3, 4), 2 + i] += so[n % 4, 1, 1, i]
        for copy in first_copies(n):
            copy.start()

    def first_add(n):
        for copy in first_copies(n):
            copy.wait_recv()
        if n >= 2:
            for copy in second_copies(n - 2):
                copy.wait_send()

        def add(i, carry):
            for h in range(2):
                own = qbuf[n % 3, h, i, x] if h == 0 else qbuf[n % 3, h, y, i]
                rbuf[n % 2, h, i] = own + s1[n % 4, h, 0, i] + s1[n % 4, h, 1, i]
            return carry

        lax.fori_loop(0, 4, add, 0)
        for copy in second_copies(n):
            copy.start()

    def finish(n):
        for copy in second_copies(n):
            copy.wait_recv()
        for h in range(2):
            own = rbuf[n % 2, h, y if h == 0 else x]
            total = own + s2[n % 4, h, 0] + s2[n % 4, h, 1] + s2[n % 4, h, 2]
            begin = DOWN_ORDER[n] * PIECE + h * 128
            lanes = slice(begin, begin + 128)
            mixed_ref[:, lanes] = (hid_ref[:, lanes].astype(F32) + total).astype(BF16)

    pieces = WIDTH // PIECE
    for n in range(pieces + 4):
        if n < pieces:
            expand(n)
        if 1 <= n < pieces + 1:
            core_add(n - 1)
        if 2 <= n < pieces + 2:
            opposite_add(n - 2)
        if 3 <= n < pieces + 3:
            first_add(n - 3)
        if n >= 4:
            finish(n - 4)

    for n in (pieces - 2, pieces - 1):
        core_copy(n).wait_send()
        for copy in second_copies(n):
            copy.wait_send()
    for n in (pieces - 3, pieces - 2, pieces - 1):
        for copy in opposite_copies(n) + first_copies(n):
            copy.wait_send()
    for copy in token_1 + token_2 + token_c:
        copy.wait_send()

    @pl.when(x != column)
    def _():
        for p in range(3):
            hand(p).wait_send()

    def drain(flow, is_down, halves):
        if is_down:
            block = wdn.at[0, pl.ds(0, 2 * halves)]
        else:
            block = wgu.at[0, pl.ds(0, 512 * halves)]
        remote(block, block, ring_s.at[flow, int(is_down)], ring_r.at[0, 0], up).wait_send()

    for is_down in (False, True):
        drain(0, is_down, 2)
        drain(1, is_down, 2)
        for flow, last in ((2, rho), (3, back)):

            @pl.when(last < 3)
            def _():
                drain(flow, is_down, 2)

            @pl.when(last == 3)
            def _():
                drain(flow, is_down, 1)


def scaled_norm(hidden_rows, norm_gain):
    values = hidden_rows.astype(F32)
    mean_square = jnp.mean(values * values, axis=-1, keepdims=True)
    return (values * lax.rsqrt(mean_square + norm_epsilon) * norm_gain.astype(F32)).astype(BF16)


def gate_table(gate_weights, routes, replica_pick, hot_experts, replica_hot):
    steps, tokens, _ = routes.shape
    lanes = jnp.arange(128, dtype=jnp.int32)
    hot_ids = jnp.arange(hot_experts.shape[0], dtype=jnp.int32)
    counts = jnp.sum((replica_hot[:, None] == hot_ids[None, :]).astype(jnp.int32), axis=0)
    copies = 1 + jnp.sum(jnp.where(hot_experts[:, None] == lanes[None, :], counts[:, None], 0), axis=0)
    gates = (gate_weights / jnp.sum(gate_weights, axis=-1, keepdims=True)).astype(BF16).astype(F32)
    here = routes[..., None] == lanes
    named = jnp.any(here, axis=2)
    pick = jnp.sum(jnp.where(here, replica_pick[..., None], 0), axis=2)
    gate = jnp.sum(jnp.where(here, gates[..., None], 0.0), axis=2)
    slot = jnp.where(named, pick % copies, -1)
    order = jnp.arange(tokens, dtype=jnp.int32)
    before = (order[None, :] < order[:, None])[None, :, :, None]
    rank = jnp.sum((before & (slot[:, None, :, :] == slot[:, :, None, :])).astype(jnp.int32), axis=2)
    return jnp.where(named & (rank < CAP), gate, 0.0).astype(BF16)


def body(
    hidden,
    norm_gain,
    gate_weights,
    routes,
    replica_pick,
    trainer_experts,
    hot_experts,
    replica_hot,
    w_gate,
    w_up,
    w_down,
    queries,
    key_cache,
    value_cache,
    new_keys,
    new_values,
    cache_lengths,
):
    steps, tokens, width = hidden.shape
    table = gate_table(gate_weights, routes, replica_pick, hot_experts, replica_hot)
    rows = jnp.concatenate([scaled_norm(hidden, norm_gain), table], axis=-1).reshape(ROWS, width + 128)
    grouped = (
        queries.reshape(steps, tokens, KV_HEADS, HEADS // KV_HEADS, HEAD)
        .transpose(1, 2, 0, 3, 4)
        .reshape(tokens, KV_HEADS, GROUP, HEAD)
    )
    pad = ((0, 0), (0, FRESH - steps), (0, 0))
    fresh_keys = jnp.pad(new_keys.transpose(1, 0, 2), pad)
    fresh_values = jnp.pad(new_values.transpose(1, 0, 2), pad)
    vmem = pl.BlockSpec(memory_space=pltpu.VMEM)
    smem = pl.BlockSpec(memory_space=pltpu.SMEM)
    hbm = pl.BlockSpec(memory_space=pl.ANY)
    dma = pltpu.SemaphoreType.DMA
    mixed, context = pl.pallas_call(
        kernel,
        out_shape=(
            jax.ShapeDtypeStruct((ROWS, width), BF16),
            jax.ShapeDtypeStruct((tokens, KV_HEADS, GROUP, HEAD), BF16),
        ),
        in_specs=[smem, smem, vmem, vmem, hbm, hbm, hbm, vmem, vmem, vmem, vmem, vmem],
        out_specs=(vmem, vmem),
        scratch_shapes=[
            pltpu.VMEM((2, WIDTH, 2 * FF), BF16),
            pltpu.VMEM((2, WIDTH // PIECE, FF, PIECE), BF16),
            pltpu.VMEM((2, 4, 4, ROWS, WIDTH + 128), BF16),
            pltpu.VMEM((2, 8, 256, 2 * FF), F32),
            pltpu.VMEM((2, 8, 256, FF), BF16),
            pltpu.VMEM((2, 8, 256, 128), F32),
            pltpu.VMEM((2, 2, 4, 4, ROWS, PIECE), F32),
            pltpu.VMEM((3, 2, 4, 4, ROWS, 128), F32),
            pltpu.VMEM((2, 2, 4, ROWS, 128), F32),
            pltpu.VMEM((4, 4, 4, ROWS, PIECE), F32),
            pltpu.VMEM((4, 2, 2, 2, ROWS, 128), F32),
            pltpu.VMEM((4, 2, 2, 4, ROWS, 128), F32),
            pltpu.VMEM((4, 2, 3, ROWS, 128), F32),
            dma((3,)),
            dma((3, 4)),
            dma((4, 2)),
            dma((4, CHUNKS)),
            dma((16,)),
            dma((16,)),
            dma((8,)),
            dma((8,)),
            dma((8, 2, 2)),
            dma((8, 2, 2)),
            dma((8, 2, 2)),
            dma((8, 2, 2)),
            dma((8, 2, 3)),
            dma((8, 2, 3)),
        ],
        compiler_params=pltpu.CompilerParams(
            collective_id=0, has_side_effects=True, vmem_limit_bytes=62 * 1024 * 1024
        ),
        cost_estimate=pl.CostEstimate(flops=20_000_000_000, bytes_accessed=8_000_000, transcendentals=3_000_000),
    )(
        trainer_experts,
        cache_lengths,
        rows,
        hidden.reshape(ROWS, width),
        w_gate,
        w_up,
        w_down,
        grouped,
        key_cache,
        value_cache,
        fresh_keys,
        fresh_values,
    )
    context = (
        context.reshape(tokens, KV_HEADS, steps, HEADS // KV_HEADS, HEAD)
        .transpose(2, 0, 1, 3, 4)
        .reshape(steps, tokens, HEADS * HEAD)
    )
    return mixed.reshape(steps, tokens, width), context


def solution(mesh):
    return jax.shard_map(
        body,
        mesh=mesh,
        in_specs=(
            P(None, ("ep", "dp"), None),
            P(),
            P(None, ("ep", "dp"), None),
            P(None, ("ep", "dp"), None),
            P(None, ("ep", "dp"), None),
            P(),
            P(),
            P(),
            P("ep", "dp", None),
            P("ep", "dp", None),
            P("ep", None, "dp"),
            P(None, ("ep", "dp"), None),
            P(("ep", "dp"), None, None),
            P(("ep", "dp"), None, None),
            P(None, ("ep", "dp"), None),
            P(None, ("ep", "dp"), None),
            P(("ep", "dp")),
        ),
        out_specs=(P(None, ("ep", "dp"), None), P(None, ("ep", "dp"), None)),
        check_vma=False,
    )
```
